32 devices in a mesh: src: 4 (over y, x), tgt: 8 (over z, core).
Axes of the slice: x: 2, y: 2, z: 4, core: 2. Of those that a mesh axis runs over, the one named last changes fastest.
Arguments:
- residual: bfloat16 [4, 512, 2304], replicated, may hold values from -6 to 6
- targets: bfloat16 [4, 2304, 512], P(None, 'tgt'), may hold values from -6 to 6
- enc_weight: bfloat16 [4, 2304, 16384], P(None, None, ('src', 'tgt')), may hold values from -0.125 to 0.125
- enc_bias: float32 [4, 16384], P(None, ('src', 'tgt')), may hold values from -3 to 3
- active: int32 [4, 512, 16384], P(None, None, ('src', 'tgt')), may hold values 0 or 1
- dec_weight: bfloat16 [40, 2304, 4096], P('src', 'tgt'), may hold values from -0.046875 to 0.046875
- dec_bias: float32 [4, 2304], P(None, 'tgt'), may hold values from -3 to 3
- tile_pairs: int32 [40, 2], P('src'), may hold values from 0 to 3, as said below
Outputs:
- dec_grad: bfloat16 [40, 2304, 4096], P('src', 'tgt')
- enc_grad: bfloat16 [4, 2304, 16384], P(None, None, ('src', 'tgt'))
- bias_grad: float32 [4, 16384], P(None, ('src', 'tgt'))
The draws below stay inside these ranges and needn't reach their ends.
Inputs may be any that keep to these rules, and one draw needn't show every extreme that they name: `tile_pairs`: rows b * 10 to (b + 1) * 10 - 1 serve latent block b; among them each pair (source, target) with source <= target appears exactly once, source in column 0 and target in column 1.
All inputs are finite; a program needn't handle non-finite values. No bound on the sum of `active` on one device may be relied on, other than what follows from the above.
Results may differ from the reference program's by a relative error of at most 0.019.
Values may be sent and summed in bfloat16 or wider, within the bound.
No kernel may reach another device: no remote copies, remote signals or barrier semaphores. Data moves between devices by JAX's collectives and lax.ppermute only.
A program may use at most 192 MiB of HBM per device.

```python
import jax
import jax.numpy as jnp
import numpy as np
from jax import lax

D = 2304
F = 16384
LAYERS = 4
TOK = 512
PAIRS = 10
ROWS = 40
BLOCK = 4096


def shuffle_pairs(subkey):
    return jax.random.permutation(subkey, PAIRS)


def draw_tile_pairs(key, part):
    listing = []
    for source in range(LAYERS):
        for target in range(source, LAYERS):
            listing.append((source, target))
    table = jnp.asarray(np.array(listing, dtype=np.int32))
    block_count = ROWS // PAIRS
    subkeys = jax.random.split(jax.random.fold_in(key, 11), block_count)
    orders = jax.vmap(shuffle_pairs)(subkeys)
    return table[orders.reshape(-1)].astype(jnp.int32)


def plant(values, stream_key, least, top_value):
    shape = values.shape
    place = [jax.random.randint(jax.random.fold_in(stream_key, axis), (), 0, shape[axis]) for axis in range(len(shape))]
    values = values.at[tuple(place)].set(least)
    longest = shape.index(max(shape))
    place[longest] = (place[longest] + 1) % shape[longest]
    return values.at[tuple(place)].set(top_value)


def block_levels(key, extent, shards, least, top_value):
    loudness, own = 1.0, jax.random.fold_in(key, 6)
    for dim, blocks in shards:
        steps = jnp.exp(jax.random.uniform(jax.random.fold_in(own, dim), (blocks,), jnp.float32, least / len(shards), top_value / len(shards)))
        loudness = loudness * jnp.repeat(steps, extent[dim] // blocks).reshape([-1 if axis == dim else 1 for axis in range(len(extent))])
    return loudness


def normal_values(rng, extent, deviation, reach, cuts=(), held_as=jnp.bfloat16):
    loudness = block_levels(rng, extent, cuts, -0.22, 0.18) if cuts else 1.0
    values = jax.random.normal(rng, extent, jnp.float32) * deviation * loudness
    return jnp.minimum(jnp.maximum(values, -reach), reach).astype(held_as)


def setup_inputs(seed: int = 0) -> dict:
    splits = jax.random.split(jax.random.key(seed), 9)
    residual = normal_values(splits[0], (LAYERS, TOK, D), 1.0, 6.0)
    targets = normal_values(splits[1], (LAYERS, D, TOK), 1.0, 6.0, ((1, 8),))
    enc_weight = normal_values(splits[2], (LAYERS, D, F), D ** -0.5, 0.125, ((2, 32),))
    enc_bias = normal_values(splits[3], (LAYERS, F), 0.5, 3.0, ((1, 32),), jnp.float32)
    active = plant((jax.random.randint(splits[4], (LAYERS, TOK, F), 0, 3) < 1).astype(jnp.int32), jax.random.fold_in(splits[4], 1), 0, 1)
    dec_weight = normal_values(splits[5], (ROWS, D, BLOCK), (F * LAYERS // 4) ** -0.5, 0.046875, ((0, 4), (1, 8)))
    dec_bias = normal_values(splits[6], (LAYERS, D), 0.5, 3.0, ((1, 8),), jnp.float32)
    tile_pairs = draw_tile_pairs(jax.random.fold_in(splits[8], 71), 0)
    return {"residual": residual, "targets": targets, "enc_weight": enc_weight, "enc_bias": enc_bias, "active": active, "dec_weight": dec_weight, "dec_bias": dec_bias, "tile_pairs": tile_pairs}


def add_layer(total, index, value):
    current = lax.dynamic_slice_in_dim(total, index, 1, 0)
    return lax.dynamic_update_slice_in_dim(total, current + value[None], index, 0)


def latent_block(latent, source, block_start, block_width):
    layer_rows = lax.dynamic_index_in_dim(latent, source, 0, keepdims=False)
    return lax.dynamic_slice_in_dim(layer_rows, block_start, block_width, 1)


def reference(residual, targets, enc_weight, enc_bias, active, dec_weight, dec_bias, tile_pairs):
    layers = residual.shape[0]
    tok_all = residual.shape[1]
    model_width = residual.shape[2]
    latents = enc_weight.shape[2]
    block_width = dec_weight.shape[2]
    mask_full = active.astype(jnp.float32)
    preact = jnp.einsum("lrd,ldf->lrf", residual.astype(jnp.float32), enc_weight.astype(jnp.float32))
    latent = ((preact + enc_bias[:, None, :]) * mask_full).astype(jnp.bfloat16)
    source_ids = tile_pairs[:, 0].astype(jnp.int32)
    target_ids = tile_pairs[:, 1].astype(jnp.int32)
    row_ids = jnp.arange(tile_pairs.shape[0], dtype=jnp.int32)
    block_starts = ((row_ids // PAIRS) * block_width).astype(jnp.int32)

    def rebuild(recon_sum, slot_data):
        weight, source, target, block_start = slot_data
        lat_block = latent_block(latent, source, block_start, block_width)
        recon_term = lax.dot_general(weight, lat_block, (((1,), (1,)), ((), ())), preferred_element_type=jnp.float32)
        return add_layer(recon_sum, target, recon_term), None

    recon_zero = jnp.zeros((layers, model_width, tok_all), jnp.float32)
    recon = lax.scan(rebuild, recon_zero, (dec_weight, source_ids, target_ids, block_starts))[0]
    recon = recon + dec_bias[:, :, None]
    error_full = (recon - targets.astype(jnp.float32)).astype(jnp.bfloat16)
    zero_index = jnp.zeros((), jnp.int32)

    def backward(grad_sum, slot_data):
        weight, source, target, block_start = slot_data
        error_rows = lax.dynamic_index_in_dim(error_full, target, 0, keepdims=False)
        lat_block = latent_block(latent, source, block_start, block_width)
        dec_term = lax.dot_general(error_rows, lat_block, (((1,), (0,)), ((), ())), preferred_element_type=jnp.float32)
        lat_term = lax.dot_general(error_rows, weight, (((0,), (0,)), ((), ())), preferred_element_type=jnp.float32)
        current = lax.dynamic_slice(grad_sum, (source, zero_index, block_start), (1, tok_all, block_width))
        grad_sum = lax.dynamic_update_slice(grad_sum, current + lat_term[None], (source, zero_index, block_start))
        return grad_sum, dec_term.astype(jnp.bfloat16)

    grad_zero = jnp.zeros((layers, tok_all, latents), jnp.float32)
    grad_sum, dec_grad = lax.scan(backward, grad_zero, (dec_weight, source_ids, target_ids, block_starts))
    pre_grad = (grad_sum * mask_full).astype(jnp.bfloat16)
    enc_grad = jnp.einsum("lrd,lrf->ldf", residual.astype(jnp.float32), pre_grad.astype(jnp.float32)).astype(jnp.bfloat16)
    bias_grad = jnp.sum(pre_grad.astype(jnp.float32), axis=1)
    return (dec_grad, enc_grad, bias_grad)
```

```python
import functools

import jax
import jax.numpy as jnp
import numpy as np
from jax import lax
from jax.experimental import pallas as pl
from jax.experimental.pallas import tpu as pltpu
from jax.sharding import PartitionSpec as P

F32 = jnp.float32
BF16 = jnp.bfloat16
NT = (((1,), (1,)), ((), ()))
NN = (((1,), (0,)), ((), ()))


def dot(a, b, dims=NN):
    return lax.dot_general(a, b, dims, preferred_element_type=F32)


def params(limit_mib):
    return pltpu.CompilerParams(vmem_limit_bytes=limit_mib * 2**20)


def pair_list(layers):
    return [(s, t) for s in range(layers) for t in range(s, layers)]


def gather_table(chips):
    table = np.full((2 * chips, 2 * chips - 1, 2), -1, np.int32)
    for me in range(2 * chips):
        chip, core = divmod(me, 2)
        way = 1 - 2 * core
        places = [(chip, core)]
        places += [(chip - way * j, core) for j in range(1, chips)]
        places += [(chip + way * j, 1 - core) for j in range(1, chips)]
        for piece, (place, order) in enumerate(places):
            if 0 <= place < chips:
                for half in range(2):
                    table[me, piece, half] = 2 * place + (order ^ half)
    return table.reshape(2 * chips, -1)


def scatter_table(chips):
    table = np.zeros((2 * chips, 3, 2 * chips), np.int32)
    last = 2 * (chips - 1)
    for me in range(2 * chips):
        chip, core = divmod(me, 2)
        way = 1 - 2 * core
        gives, keeps = [], []
        for dist in range(chips - 1, 0, -1):
            slot = 2 * (chips - 1 - dist)
            for half in range(2):
                if 0 <= chip - way * dist < chips:
                    gives.append((2 * (chip - way * dist) + ((1 - core) ^ half), slot + half))
                if 0 <= chip + way * dist < chips:
                    keeps.append((2 * (chip + way * dist) + (core ^ half), slot + half))
        gives.append((2 * chip + 1 - core, last))
        keeps.append((2 * chip + core, last))
        for step, (tile, slot) in enumerate(gives):
            table[me, :, step] = (tile, slot, keeps[0][1])
        for step, (tile, slot) in enumerate(keeps):
            table[me, :, len(gives) + step] = (tile, gives[-1][1], slot)
    return table.reshape(2 * chips, -1)


def encode_kernel(res_ref, weight_ref, bias_ref, active_ref, out_ref):
    pre = dot(res_ref[0], weight_ref[0]) + bias_ref[0]
    out_ref[0] = (pre * active_ref[0].astype(F32)).astype(BF16)


def encode(residual, enc_weight, bias, active, start, rows):
    layers, _, width = residual.shape
    own = enc_weight.shape[2]
    at = start // rows
    return pl.pallas_call(
        encode_kernel,
        grid=(layers,),
        in_specs=[
            pl.BlockSpec((1, rows, width), lambda s: (s, at, 0)),
            pl.BlockSpec((1, width, own), lambda s: (s, 0, 0)),
            pl.BlockSpec((1, 1, own), lambda s: (s, 0, 0)),
            pl.BlockSpec((1, rows, own), lambda s: (s, at, 0)),
        ],
        out_specs=pl.BlockSpec((1, rows, own), lambda s: (s, 0, 0)),
        out_shape=jax.ShapeDtypeStruct((layers, rows, own), BF16),
        compiler_params=params(32),
        name="encode",
    )(residual, enc_weight, bias, active)


def recon_kernel(pairs, pieces, layers, start, aliased, meta, *refs):
    npairs = len(pairs)
    weights = refs[:npairs]
    piece_refs = refs[npairs : npairs + pieces]
    rest = refs[npairs + pieces + aliased :]
    low_ref, high_ref, lat_out, lat, total, in_sem, out_sem = rest
    step = pl.program_id(0)
    rows = lat.shape[2]

    def fetch(piece, half):
        slot = meta[npairs + 2 * piece + half]
        return slot, pltpu.make_async_copy(
            piece_refs[piece].at[half], lat.at[jnp.maximum(slot, 0)], in_sem.at[2 * piece + half]
        )

    def keep():
        return pltpu.make_async_copy(lat, lat_out.at[:, :, pl.ds(start, rows)], out_sem)

    @pl.when(step == 0)
    def _():
        for piece in range(pieces):
            for half in range(2):
                slot, copy = fetch(piece, half)
                pl.when(slot >= 0)(copy.start)
        total[...] = jnp.zeros_like(total)
        for piece in range(pieces):
            for half in range(2):
                slot, copy = fetch(piece, half)
                pl.when(slot >= 0)(copy.wait)
        keep().start()

    for t in range(layers):
        term = total[t]
        for p, (source, target) in enumerate(pairs):
            if target == t:
                term = term + dot(weights[p][0], lat[step, source], NT)
        total[t] = term

    @pl.when(step == pl.num_programs(0) - 1)
    def _():
        half = low_ref.shape[0]
        low_ref[...] = total[:half].astype(BF16)
        high_ref[...] = total[half:].astype(BF16)
        keep().wait()


def weight_specs(npairs, feat, own, column):
    return [
        pl.BlockSpec((1, feat, own), functools.partial(lambda p, i, meta: (meta[p], 0, column(i, meta)), p))
        for p in range(npairs)
    ]


def recon(meta, dec_weight, pieces, lat_all, tok, start):
    npairs, feat, cols = dec_weight.shape
    _, layers, rows, own = pieces[0].shape
    tiles = cols // own
    pairs = pair_list(layers)
    any_spec = pl.BlockSpec(memory_space=pl.ANY)
    half = layers // 2
    extra = [] if lat_all is None else [lat_all]
    outs = (
        jax.ShapeDtypeStruct((half, feat, rows), BF16),
        jax.ShapeDtypeStruct((layers - half, feat, rows), BF16),
        jax.ShapeDtypeStruct((tiles, layers, tok, own), BF16),
    )
    return pl.pallas_call(
        functools.partial(recon_kernel, pairs, len(pieces), layers, start, len(extra)),
        grid_spec=pltpu.PrefetchScalarGridSpec(
            num_scalar_prefetch=1,
            grid=(tiles,),
            in_specs=weight_specs(npairs, feat, own, lambda i, meta: i) + [any_spec] * (len(pieces) + len(extra)),
            out_specs=[
                pl.BlockSpec(outs[0].shape, lambda i, meta: (0, 0, 0)),
                pl.BlockSpec(outs[1].shape, lambda i, meta: (0, 0, 0)),
                any_spec,
            ],
            scratch_shapes=[
                pltpu.VMEM((tiles, layers, rows, own), BF16),
                pltpu.VMEM((layers, feat, rows), F32),
                pltpu.SemaphoreType.DMA((2 * len(pieces),)),
                pltpu.SemaphoreType.DMA,
            ],
        ),
        out_shape=outs,
        input_output_aliases={} if lat_all is None else {1 + npairs + len(pieces): 2},
        compiler_params=params(40),
        cost_estimate=pl.CostEstimate(
            flops=2 * npairs * feat * cols * rows, bytes_accessed=2 * npairs * feat * cols, transcendentals=0
        ),
        name="recon",
    )(meta, *([dec_weight] * npairs), *pieces, *extra)


def grad_kernel(pairs, layers, aliased, meta, *refs):
    npairs = len(pairs)
    weights = refs[:npairs]
    low_ref, high_ref, bias_ref, target_ref = refs[npairs : npairs + 4]
    give_ref, keep_ref, error_out, error_t, error_rest = refs[npairs + 4 + aliased :]
    step = pl.program_id(0)
    feat, rows = target_ref.shape[1:]
    main = feat // 256 * 256
    rest = feat - main

    @pl.when(step == 0)
    def _():
        half = low_ref.shape[0]
        for t in range(layers):
            whole = low_ref[t] if t < half else high_ref[t - half]
            error = (whole.astype(F32) + bias_ref[t] - target_ref[t].astype(F32)).astype(BF16)
            error_out[t] = error
            turned = error.astype(F32).T.astype(BF16)
            if main:
                error_t[t] = turned[:, :main]
            if rest:
                for s in range(layers):
                    piece = turned[:, main:]
                    error_rest[s, :, t * rest : (t + 1) * rest] = piece if t >= s else jnp.zeros_like(piece)

    tiles = []
    for s in range(layers):
        total = None
        mine = [(p, t) for p, (source, t) in enumerate(pairs) if source == s]
        if main:
            for p, t in mine:
                term = dot(error_t[t], weights[p][0, :main])
                total = term if total is None else total + term
        if rest:
            stack = [weights[p][0, main:] for p, _ in mine]
            term = dot(error_rest[s][:, s * rest :], jnp.concatenate(stack, 0))
            total = term if total is None else total + term
        tiles.append(total.astype(BF16))

    gives = meta[npairs + 3 * pl.num_programs(0)]

    @pl.when(step < gives)
    def _():
        for s in range(layers):
            give_ref[0, s] = tiles[s]

    @pl.when(step >= gives)
    def _():
        for s in range(layers):
            keep_ref[0, s] = tiles[s]


def grad(meta, dec_weight, low, high, bias, targets, error_all, start, own):
    npairs, feat, cols = dec_weight.shape
    layers, _, tok = targets.shape
    rows = low.shape[2]
    tiles = cols // own
    pairs = pair_list(layers)
    main = feat // 256 * 256
    rest = feat - main
    at = start // rows
    extra = [] if error_all is None else [error_all]
    slots = jax.ShapeDtypeStruct((tiles - 1, layers, rows, own), BF16)
    outs = (slots, slots, jax.ShapeDtypeStruct((layers, feat, tok), BF16))
    whole = lambda shape: pl.BlockSpec(shape, lambda i, meta: (0,) * len(shape))
    return pl.pallas_call(
        functools.partial(grad_kernel, pairs, layers, len(extra)),
        grid_spec=pltpu.PrefetchScalarGridSpec(
            num_scalar_prefetch=1,
            grid=(tiles,),
            in_specs=weight_specs(npairs, feat, own, lambda i, meta: meta[npairs + i])
            + [
                whole(low.shape),
                whole(high.shape),
                whole(bias.shape),
                pl.BlockSpec((layers, feat, rows), lambda i, meta: (0, 0, at)),
            ]
            + [pl.BlockSpec(memory_space=pl.ANY)] * len(extra),
            out_specs=[
                pl.BlockSpec((1, layers, rows, own), lambda i, meta: (meta[npairs + tiles + i], 0, 0, 0)),
                pl.BlockSpec((1, layers, rows, own), lambda i, meta: (meta[npairs + 2 * tiles + i], 0, 0, 0)),
                pl.BlockSpec((layers, feat, rows), lambda i, meta: (0, 0, at)),
            ],
            scratch_shapes=[
                pltpu.VMEM((layers, rows, max(main, 128)), BF16),
                pltpu.VMEM((layers, rows, max(layers * rest, 128)), BF16),
            ],
        ),
        out_shape=outs,
        input_output_aliases={} if error_all is None else {1 + npairs + 4: 2},
        compiler_params=params(40),
        cost_estimate=pl.CostEstimate(
            flops=2 * npairs * feat * cols * rows, bytes_accessed=2 * npairs * feat * cols, transcendentals=0
        ),
        name="latent_grad",
    )(meta, *([dec_weight] * npairs), low, high, bias, targets, *extra)


def dec_grad_kernel(meta, sources, targets, error_ref, lat_ref, out_ref):
    own = lat_ref.shape[3]
    for tile in range(lat_ref.shape[0]):
        out_ref[0, :, tile * own : (tile + 1) * own] = dot(error_ref[0], lat_ref[tile, 0]).astype(BF16)


def decoder_grad(perm, error_all, lat_all):
    layers, feat, tok = error_all.shape
    tiles, _, _, own = lat_all.shape
    pairs = pair_list(layers)
    npairs = len(pairs)
    sources = jnp.asarray(np.array([s for s, _ in pairs], np.int32))
    targets = jnp.asarray(np.array([t for _, t in pairs], np.int32))
    return pl.pallas_call(
        dec_grad_kernel,
        grid_spec=pltpu.PrefetchScalarGridSpec(
            num_scalar_prefetch=3,
            grid=(npairs,),
            in_specs=[
                pl.BlockSpec((1, feat, tok), lambda p, m, s, t: (t[p], 0, 0)),
                pl.BlockSpec((tiles, 1, tok, own), lambda p, m, s, t: (0, s[p], 0, 0)),
            ],
            out_specs=pl.BlockSpec((1, feat, tiles * own), lambda p, m, s, t: (m[p], 0, 0)),
        ),
        out_shape=jax.ShapeDtypeStruct((npairs, feat, tiles * own), BF16),
        compiler_params=params(40),
        cost_estimate=pl.CostEstimate(
            flops=2 * npairs * feat * tok * tiles * own, bytes_accessed=2 * npairs * feat * tiles * own, transcendentals=0
        ),
        name="dec_grad",
    )(perm, sources, targets, error_all, lat_all)


def enc_grad_kernel(parts, *refs):
    res_ref = refs[0]
    grads = refs[1 : 1 + parts]
    out_ref, bias_ref = refs[1 + parts :]
    whole = jnp.concatenate([g[0] for g in grads], 0)
    out_ref[0] = dot(res_ref[0], whole).astype(BF16)
    bias_ref[0] = jnp.sum(whole.astype(F32), axis=0, keepdims=True)


def encoder_grad(residual_t, grads):
    layers, width, tok = residual_t.shape
    _, rows, own = grads[0].shape
    return pl.pallas_call(
        functools.partial(enc_grad_kernel, len(grads)),
        grid=(layers,),
        in_specs=[pl.BlockSpec((1, width, tok), lambda s: (s, 0, 0))]
        + [pl.BlockSpec((1, rows, own), lambda s: (s, 0, 0))] * len(grads),
        out_specs=[
            pl.BlockSpec((1, width, own), lambda s: (s, 0, 0)),
            pl.BlockSpec((1, 1, own), lambda s: (s, 0, 0)),
        ],
        out_shape=(
            jax.ShapeDtypeStruct((layers, width, own), BF16),
            jax.ShapeDtypeStruct((layers, 1, own), F32),
        ),
        compiler_params=params(40),
        name="enc_grad",
    )(residual_t, *grads)


def swap_cores(value, devices):
    return lax.ppermute(value, "tgt", [(i, i ^ 1) for i in range(devices)])


def hop(value, chips, first):
    perm = []
    for chip in first:
        if chip + 1 < chips:
            perm.append((2 * chip, 2 * chip + 2))
            other = chips - 1 - chip
            perm.append((2 * other + 1, 2 * other - 1))
    return lax.ppermute(value, "tgt", perm)


def add(*values):
    total = values[0].astype(F32)
    for value in values[1:]:
        total = total + value.astype(F32)
    return total.astype(BF16)


def sum_over_src(value, size, bits):
    if size & (size - 1):
        return lax.psum(value, "src")
    for bit in bits:
        value = add(value, lax.ppermute(value, "src", [(i, i ^ (1 << bit)) for i in range(size)]))
    return value


def shards(blocks, devices, residual, targets, enc_weight, enc_bias, active, dec_weight, dec_bias, tile_pairs):
    layers, tok, _ = residual.shape
    own = enc_weight.shape[2]
    chips = devices // 2
    rows = 128
    starts = list(range(0, tok, rows))
    pairs = np.array(pair_list(layers), np.int32)
    me = lax.axis_index("tgt")

    same = jnp.all(tile_pairs[None, :, :] == pairs[:, None, :], axis=2)
    perm = jnp.sum(jnp.where(same, jnp.arange(len(pairs), dtype=jnp.int32)[None, :], 0), axis=1, dtype=jnp.int32)
    chip, core = me // 2, me % 2
    gives = 1 + 2 * jnp.where(core == 0, chip, chips - 1 - chip)
    gather_meta = jnp.concatenate([perm, jnp.asarray(gather_table(chips))[me]])
    scatter_meta = jnp.concatenate([perm, jnp.asarray(scatter_table(chips))[me], gives[None].astype(jnp.int32)])
    enc_bias3 = enc_bias[:, None, :]
    dec_bias3 = dec_bias[:, :, None]
    residual_t = jnp.swapaxes(residual, 1, 2)
    bits = [b for b in range(blocks.bit_length()) if (1 << b) < blocks]

    lat_all = error_all = None
    grads = []
    for start in starts:
        mine = encode(residual, enc_weight, enc_bias3, active, start, rows)
        block = jnp.stack([mine, swap_cores(mine, devices)])
        moved = [block]
        for j in range(1, chips):
            moved.append(hop(moved[-1], chips, range(j - 1, chips - 1)))
        pieces = moved + [swap_cores(value, devices) for value in moved[1:]]
        low, high, lat_all = recon(gather_meta, dec_weight, pieces, lat_all, tok, start)
        low = sum_over_src(low, blocks, bits)
        high = sum_over_src(high, blocks, bits[::-1])
        give, keep, error_all = grad(scatter_meta, dec_weight, low, high, dec_bias3, targets, error_all, start, own)
        given = swap_cores(give, devices)
        last = 2 * (chips - 1)
        carry = None
        for j in range(1, chips):
            at = slice(2 * (j - 1), 2 * j)
            terms = [keep[at], given[at]] + ([] if carry is None else [carry])
            carry = hop(add(*terms), chips, range(0, j))
        total = sum(v.astype(F32) for v in (keep[last], given[last], carry[0], swap_cores(carry[1], devices)))
        grads.append((total * active[:, start : start + rows].astype(F32)).astype(BF16))

    dec_grad = decoder_grad(perm, error_all, lat_all)
    enc_grad, bias_grad = encoder_grad(residual_t, grads)
    return (dec_grad, enc_grad, bias_grad[:, 0])


def solution(mesh):
    in_specs = (
        P(),
        P(None, "tgt", None),
        P(None, None, ("src", "tgt")),
        P(None, ("src", "tgt")),
        P(None, None, ("src", "tgt")),
        P("src", "tgt", None),
        P(None, "tgt"),
        P("src", None),
    )
    out_specs = (P("src", "tgt", None), P(None, None, ("src", "tgt")), P(None, ("src", "tgt")))
    body = functools.partial(shards, mesh.shape["src"], mesh.shape["tgt"])
    return jax.shard_map(body, mesh=mesh, in_specs=in_specs, out_specs=out_specs, check_vma=False)
```

```python
import functools

import jax
import jax.numpy as jnp
import numpy as np
from jax import lax
from jax.experimental import pallas as pl
from jax.experimental.pallas import tpu as pltpu
from jax.sharding import PartitionSpec as P

F32 = jnp.float32
BF16 = jnp.bfloat16
NT = (((1,), (1,)), ((), ()))
NN = (((1,), (0,)), ((), ()))


def dot(a, b, dims=NN):
    return lax.dot_general(a, b, dims, preferred_element_type=F32)


def params(limit_mib):
    return pltpu.CompilerParams(vmem_limit_bytes=limit_mib * 2**20)


VMEM_MIB = 56
LIGHT = pl.CostEstimate(flops=1, bytes_accessed=1, transcendentals=0)


def pair_list(layers):
    return [(s, t) for s in range(layers) for t in range(s, layers)]


def gather_table(chips):
    table = np.full((2 * chips, 2 * chips - 1, 2), -1, np.int32)
    for me in range(2 * chips):
        chip, core = divmod(me, 2)
        way = 1 - 2 * core
        places = [(chip, core)]
        places += [(chip - way * j, core) for j in range(1, chips)]
        places += [(chip + way * j, 1 - core) for j in range(1, chips)]
        for piece, (place, order) in enumerate(places):
            if 0 <= place < chips:
                for half in range(2):
                    table[me, piece, half] = 2 * place + (order ^ half)
    return table.reshape(2 * chips, -1)


def scatter_table(chips):
    table = np.zeros((2 * chips, 3, 2 * chips), np.int32)
    last = 2 * (chips - 1)
    for me in range(2 * chips):
        chip, core = divmod(me, 2)
        way = 1 - 2 * core
        gives, keeps = [], []
        for dist in range(chips - 1, 0, -1):
            slot = 2 * (chips - 1 - dist)
            for half in range(2):
                if 0 <= chip - way * dist < chips:
                    gives.append((2 * (chip - way * dist) + ((1 - core) ^ half), slot + half))
                if 0 <= chip + way * dist < chips:
                    keeps.append((2 * (chip + way * dist) + (core ^ half), slot + half))
        gives.append((2 * chip + 1 - core, last))
        keeps.append((2 * chip + core, last))
        for step, (tile, slot) in enumerate(gives):
            table[me, :, step] = (tile, slot, keeps[0][1])
        for step, (tile, slot) in enumerate(keeps):
            table[me, :, len(gives) + step] = (tile, gives[-1][1], slot)
    return table.reshape(2 * chips, -1)


def encode_kernel(res_ref, weight_ref, bias_ref, active_ref, out_ref):
    pre = dot(res_ref[0], weight_ref[0]) + bias_ref[pl.ds(pl.program_id(0), 1)]
    out_ref[0] = (pre * active_ref[0].astype(F32)).astype(BF16)


def encode(residual, enc_weight, bias, active, start, rows):
    layers, _, width = residual.shape
    own = enc_weight.shape[2]
    at = start // rows
    return pl.pallas_call(
        encode_kernel,
        grid=(layers,),
        in_specs=[
            pl.BlockSpec((1, rows, width), lambda s: (s, at, 0)),
            pl.BlockSpec((1, width, own), lambda s: (s, 0, 0)),
            pl.BlockSpec((layers, own), lambda s: (0, 0)),
            pl.BlockSpec((1, rows, own), lambda s: (s, at, 0)),
        ],
        out_specs=pl.BlockSpec((1, rows, own), lambda s: (s, 0, 0)),
        out_shape=jax.ShapeDtypeStruct((layers, rows, own), BF16),
        compiler_params=params(VMEM_MIB),
        cost_estimate=LIGHT,
        name="encode",
    )(residual, enc_weight, bias, active)


def recon_sum(pairs, weights, lat_tile, total):
    for t in range(total.shape[0]):
        term = total[t]
        for p, (source, target) in enumerate(pairs):
            if target == t:
                term = term + dot(weights[p][0], lat_tile(source), NT)
        total[t] = term


def recon_ends(low_ref, high_ref, total):
    @pl.when(pl.program_id(0) == pl.num_programs(0) - 1)
    def _():
        half = low_ref.shape[0]
        low_ref[...] = total[:half].astype(BF16)
        high_ref[...] = total[half:].astype(BF16)


def recon_whole_kernel(pairs, meta, *refs):
    weights = refs[: len(pairs)]
    lat_ref, low_ref, high_ref, total = refs[len(pairs) :]

    @pl.when(pl.program_id(0) == 0)
    def _():
        total[...] = jnp.zeros_like(total)

    recon_sum(pairs, weights, lambda source: lat_ref[0, source], total)
    recon_ends(low_ref, high_ref, total)


def recon_pieces_kernel(pairs, pieces, meta, *refs):
    npairs = len(pairs)
    weights = refs[:npairs]
    piece_refs = refs[npairs : npairs + pieces]
    low_ref, high_ref, lat_out, lat, total, in_sem, out_sem = refs[npairs + pieces :]
    step = pl.program_id(0)

    def fetch(piece, half):
        slot = meta[npairs + 2 * piece + half]
        return slot, pltpu.make_async_copy(
            piece_refs[piece].at[half], lat.at[jnp.maximum(slot, 0)], in_sem.at[2 * piece + half]
        )

    def keep():
        return pltpu.make_async_copy(lat, lat_out, out_sem)

    @pl.when(step == 0)
    def _():
        for piece in range(pieces):
            for half in range(2):
                slot, copy = fetch(piece, half)
                pl.when(slot >= 0)(copy.start)
        total[...] = jnp.zeros_like(total)
        for piece in range(pieces):
            for half in range(2):
                slot, copy = fetch(piece, half)
                pl.when(slot >= 0)(copy.wait)
        keep().start()

    recon_sum(pairs, weights, lambda source: lat[step, source], total)
    recon_ends(low_ref, high_ref, total)

    @pl.when(step == pl.num_programs(0) - 1)
    def _():
        keep().wait()


def weight_specs(npairs, feat, own, column):
    return [
        pl.BlockSpec((1, feat, own), functools.partial(lambda p, i, meta: (meta[p], 0, column(i, meta)), p))
        for p in range(npairs)
    ]


def recon(meta, dec_weight, lat):
    npairs, feat, cols = dec_weight.shape
    gathered = not isinstance(lat, list)
    *_, layers, rows, own = lat.shape if gathered else lat[0].shape
    tiles = cols // own
    pairs = pair_list(layers)
    half = layers // 2
    any_spec = pl.BlockSpec(memory_space=pl.ANY)
    outs = [
        jax.ShapeDtypeStruct((half, feat, rows), BF16),
        jax.ShapeDtypeStruct((layers - half, feat, rows), BF16),
    ]
    out_specs = [pl.BlockSpec(o.shape, lambda i, meta: (0, 0, 0)) for o in outs]
    scratch = [pltpu.VMEM((layers, feat, rows), F32)]
    if gathered:
        body = functools.partial(recon_whole_kernel, pairs)
        lat_specs = [pl.BlockSpec((1, layers, rows, own), lambda i, meta: (i, 0, 0, 0))]
    else:
        body = functools.partial(recon_pieces_kernel, pairs, len(lat))
        lat_specs = [any_spec] * len(lat)
        outs.append(jax.ShapeDtypeStruct((tiles, layers, rows, own), BF16))
        out_specs.append(any_spec)
        scratch = (
            [pltpu.VMEM((tiles, layers, rows, own), BF16)]
            + scratch
            + [pltpu.SemaphoreType.DMA((2 * len(lat),)), pltpu.SemaphoreType.DMA]
        )
    return pl.pallas_call(
        body,
        grid_spec=pltpu.PrefetchScalarGridSpec(
            num_scalar_prefetch=1,
            grid=(tiles,),
            in_specs=weight_specs(npairs, feat, own, lambda i, meta: i) + lat_specs,
            out_specs=out_specs,
            scratch_shapes=scratch,
        ),
        out_shape=outs,
        compiler_params=params(VMEM_MIB),
        cost_estimate=LIGHT,
        name="recon",
    )(meta, *([dec_weight] * npairs), *([lat] if gathered else lat))


def grad_kernel(pairs, layers, split, meta, *refs):
    npairs = len(pairs)
    weights = refs[:npairs]
    low_ref, high_ref, bias_ref, target_ref = refs[npairs : npairs + 4]
    outs = refs[npairs + 4 : -3]
    error_out, error_t, error_rest = refs[-3:]
    step = pl.program_id(0)
    feat, rows = target_ref.shape[1:]
    main = feat // 256 * 256
    rest = feat - main

    @pl.when(step == 0)
    def _():
        half = low_ref.shape[0]
        for t in range(layers):
            whole = low_ref[t] if t < half else high_ref[t - half]
            error = (whole.astype(F32) + bias_ref[t] - target_ref[t].astype(F32)).astype(BF16)
            error_out[t] = error
            turned = error.astype(F32).T.astype(BF16)
            if main:
                error_t[t] = turned[:, :main]
            if rest:
                for s in range(layers):
                    piece = turned[:, main:]
                    error_rest[s, :, t * rest : (t + 1) * rest] = piece if t >= s else jnp.zeros_like(piece)

    tiles = []
    for s in range(layers):
        total = None
        mine = [(p, t) for p, (source, t) in enumerate(pairs) if source == s]
        if main:
            for p, t in mine:
                term = dot(error_t[t], weights[p][0, :main])
                total = term if total is None else total + term
        if rest:
            stack = [weights[p][0, main:] for p, _ in mine]
            term = dot(error_rest[s][:, s * rest :], jnp.concatenate(stack, 0))
            total = term if total is None else total + term
        tiles.append(total.astype(BF16))

    def write(out_ref):
        for s in range(layers):
            out_ref[0, s] = tiles[s]

    if split:
        gives = meta[npairs + 3 * pl.num_programs(0)]
        early = meta[npairs + pl.num_programs(0) + step] < 2
        pl.when((step < gives) & early)(functools.partial(write, outs[0]))
        pl.when((step < gives) & ~early)(functools.partial(write, outs[1]))
        pl.when(step >= gives)(functools.partial(write, outs[2]))
    else:
        write(outs[0])


def grad(meta, dec_weight, low, high, bias, targets, own, split):
    npairs, feat, cols = dec_weight.shape
    layers, _, rows = targets.shape
    tiles = cols // own
    pairs = pair_list(layers)
    main = feat // 256 * 256
    rest = feat - main
    block = (1, layers, rows, own)
    if split:
        outs = [jax.ShapeDtypeStruct((count, layers, rows, own), BF16) for count in (2, tiles - 3, tiles - 1)]
        out_specs = [
            pl.BlockSpec(block, lambda i, meta: (jnp.minimum(meta[npairs + tiles + i], 1), 0, 0, 0)),
            pl.BlockSpec(block, lambda i, meta: (jnp.maximum(meta[npairs + tiles + i] - 2, 0), 0, 0, 0)),
            pl.BlockSpec(block, lambda i, meta: (meta[npairs + 2 * tiles + i], 0, 0, 0)),
        ]
        column = lambda i, meta: meta[npairs + i]
    else:
        outs = [jax.ShapeDtypeStruct((tiles, layers, rows, own), BF16)]
        out_specs = [pl.BlockSpec(block, lambda i, meta: (i, 0, 0, 0))]
        column = lambda i, meta: i
    whole = lambda shape: pl.BlockSpec(shape, lambda i, meta: (0,) * len(shape))
    return pl.pallas_call(
        functools.partial(grad_kernel, pairs, layers, split),
        grid_spec=pltpu.PrefetchScalarGridSpec(
            num_scalar_prefetch=1,
            grid=(tiles,),
            in_specs=weight_specs(npairs, feat, own, column)
            + [
                whole(low.shape),
                whole(high.shape),
                whole(bias.shape),
                whole(targets.shape),
            ],
            out_specs=out_specs + [whole((layers, feat, rows))],
            scratch_shapes=[
                pltpu.VMEM((layers, rows, max(main, 128)), BF16),
                pltpu.VMEM((layers, rows, max(layers * rest, 128)), BF16),
            ],
        ),
        out_shape=outs + [jax.ShapeDtypeStruct((layers, feat, rows), BF16)],
        compiler_params=params(VMEM_MIB),
        cost_estimate=LIGHT,
        name="latent_grad",
    )(meta, *([dec_weight] * npairs), low, high, bias, targets)


def dec_grad_kernel(pairs, parts, perm, *refs):
    errors, lats, out_ref = refs[:parts], refs[parts : 2 * parts], refs[-1]
    for p, (source, target) in enumerate(pairs):
        total = None
        for error, lat in zip(errors, lats):
            term = dot(error[target], lat[0, source])
            total = term if total is None else total + term
        out_ref[perm[p]] = total.astype(BF16)


def decoder_grad(perm, errors, lats):
    layers, feat, _ = errors[0].shape
    tiles, _, _, own = lats[0].shape
    pairs = pair_list(layers)
    npairs = len(pairs)
    return pl.pallas_call(
        functools.partial(dec_grad_kernel, pairs, len(errors)),
        grid_spec=pltpu.PrefetchScalarGridSpec(
            num_scalar_prefetch=1,
            grid=(tiles,),
            in_specs=[pl.BlockSpec(e.shape, lambda i, m: (0, 0, 0)) for e in errors]
            + [pl.BlockSpec((1,) + lat.shape[1:], lambda i, m: (i, 0, 0, 0)) for lat in lats],
            out_specs=pl.BlockSpec((npairs, feat, own), lambda i, m: (0, 0, i)),
        ),
        out_shape=jax.ShapeDtypeStruct((npairs, feat, tiles * own), BF16),
        compiler_params=params(VMEM_MIB),
        cost_estimate=LIGHT,
        name="dec_grad",
    )(perm, *errors, *lats)


def enc_grad_kernel(parts, res_ref, *refs):
    last_ref, active_ref, out_ref, bias_ref = refs[parts:]
    last = (last_ref[0].astype(F32) * active_ref[0].astype(F32)).astype(BF16)
    whole = jnp.concatenate([part[0] for part in refs[:parts]] + [last], 0)
    out_ref[0] = dot(res_ref[0], whole).astype(BF16)
    bias_ref[pl.ds(pl.program_id(0), 1)] = jnp.sum(whole.astype(F32), axis=0, keepdims=True)


def encoder_grad(residual_t, grads, last, active, start):
    layers, width, tok = residual_t.shape
    _, rows, own = last.shape
    at = start // rows
    part = lambda value: pl.BlockSpec((1,) + value.shape[1:], lambda s: (s, 0, 0))
    return pl.pallas_call(
        functools.partial(enc_grad_kernel, len(grads)),
        grid=(layers,),
        in_specs=[part(residual_t)]
        + [part(g) for g in grads]
        + [part(last), pl.BlockSpec((1, rows, own), lambda s: (s, at, 0))],
        out_specs=[
            pl.BlockSpec((1, width, own), lambda s: (s, 0, 0)),
            pl.BlockSpec((layers, own), lambda s: (0, 0)),
        ],
        out_shape=(
            jax.ShapeDtypeStruct((layers, width, own), BF16),
            jax.ShapeDtypeStruct((layers, own), F32),
        ),
        compiler_params=params(24),
        cost_estimate=LIGHT,
        name="enc_grad",
    )(residual_t, *grads, last, active)


def swap_cores(value, devices):
    return lax.ppermute(value, "tgt", [(i, i ^ 1) for i in range(devices)])


def hop(value, chips, first):
    perm = []
    for chip in first:
        if chip + 1 < chips:
            perm.append((2 * chip, 2 * chip + 2))
            other = chips - 1 - chip
            perm.append((2 * other + 1, 2 * other - 1))
    return lax.ppermute(value, "tgt", perm)


def after(value, *others):
    return lax.optimization_barrier((value,) + others)[0]


def add(*values):
    total = values[0].astype(F32)
    for value in values[1:]:
        total = total + value.astype(F32)
    return total.astype(BF16)


def sum_over_src(value, size, bits):
    if size & (size - 1):
        return lax.psum(value, "src")
    for bit in bits:
        value = add(value, lax.ppermute(value, "src", [(i, i ^ (1 << bit)) for i in range(size)]))
    return value


def token_chunks(tok):
    parts = [4, 2, 2]
    unit = tok // sum(parts)
    return [(unit * sum(parts[:i]), unit * part) for i, part in enumerate(parts)]


def shards(blocks, devices, residual, targets, enc_weight, enc_bias, active, dec_weight, dec_bias, tile_pairs):
    layers, tok, _ = residual.shape
    own = enc_weight.shape[2]
    chips = devices // 2
    chunks = token_chunks(tok)
    pairs = np.array(pair_list(layers), np.int32)
    me = lax.axis_index("tgt")

    same = jnp.all(tile_pairs[None, :, :] == pairs[:, None, :], axis=2)
    perm = jnp.sum(jnp.where(same, jnp.arange(len(pairs), dtype=jnp.int32)[None, :], 0), axis=1, dtype=jnp.int32)
    chip, core = me // 2, me % 2
    gives = 1 + 2 * jnp.where(core == 0, chip, chips - 1 - chip)
    scatter_meta = jnp.concatenate([perm, jnp.asarray(scatter_table(chips))[me], gives[None].astype(jnp.int32)])
    dec_bias3 = dec_bias[:, :, None]
    residual_t = jnp.swapaxes(residual, 1, 2)
    bits = [b for b in range(blocks.bit_length()) if (1 << b) < blocks]

    def scatter(slots):
        early, rest, keep = slots
        early, rest = swap_cores(early, devices), swap_cores(rest, devices)
        last = 2 * (chips - 1)
        gate, carry = [], None
        for j in range(1, chips):
            at = slice(2 * (j - 1), 2 * j)
            terms = [keep[at], early if j == 1 else rest[2 * j - 4 : 2 * j - 2]]
            terms += [] if carry is None else [after(carry, *gate)]
            carry = hop(add(*terms), chips, range(0, j))
            gate = yield carry
            gate = gate or []
        total = add(keep[last], rest[last - 2], carry[0], swap_cores(carry[1], devices))
        while True:
            yield total

    order, lats, parts = [], [], []
    for start, rows in chunks:
        block = encode(after(residual, *order), enc_weight, enc_bias, active, start, rows)
        order = [block]
        lats.append(lax.all_gather(block, "tgt", axis=0))
        parts.append(targets[:, :, start : start + rows])
    order += [residual_t] + parts

    errors, running = [], []
    final = len(chunks) - 1
    for c in range(final + 1):
        order += [next(steps) for steps in running[: max(c - 1, 0)]]
        low, high = recon(perm, dec_weight, after(lats[c], *order))
        order = [low, high]
        order += [next(steps) for steps in running[: c if c == final else max(c - 1, 0)]]
        low = sum_over_src(low, blocks, bits)
        high = sum_over_src(high, blocks, bits[::-1])
        *slots, error = grad(scatter_meta, dec_weight, after(low, *order), high, dec_bias3, parts[c], own, c < final)
        errors.append(error)
        order = [error]
        if c < final:
            running.append(scatter(slots))
    last = lax.psum_scatter(slots[0], "tgt", scatter_dimension=0)
    values = [next(steps, None) for steps in running]
    dec_grad = decoder_grad(after(perm, *order), errors, lats)
    grads = []
    for c, (steps, value) in enumerate(zip(running, values)):
        if value.ndim == 4:
            value = steps.send([dec_grad])
        while value.ndim == 4:
            value = next(steps)
        start, rows = chunks[c]
        grads.append((value.astype(F32) * active[:, start : start + rows].astype(F32)).astype(BF16))
    last = after(last, dec_grad)
    enc_grad, bias_grad = encoder_grad(residual_t, grads, last, active, chunks[-1][0])
    return (dec_grad, enc_grad, bias_grad)


def solution(mesh):
    in_specs = (
        P(),
        P(None, "tgt", None),
        P(None, None, ("src", "tgt")),
        P(None, ("src", "tgt")),
        P(None, None, ("src", "tgt")),
        P("src", "tgt", None),
        P(None, "tgt"),
        P("src", None),
    )
    out_specs = (P("src", "tgt", None), P(None, None, ("src", "tgt")), P(None, ("src", "tgt")))
    body = functools.partial(shards, mesh.shape["src"], mesh.shape["tgt"])
    return jax.shard_map(body, mesh=mesh, in_specs=in_specs, out_specs=out_specs, check_vma=False)
```

```python
import functools
import math

import jax
import jax.numpy as jnp
import numpy as np
from jax import lax
from jax.experimental import pallas as pl
from jax.experimental.pallas import tpu as pltpu
from jax.sharding import PartitionSpec as P

F32 = jnp.float32
BF16 = jnp.bfloat16
NT = (((1,), (1,)), ((), ()))
NN = (((1,), (0,)), ((), ()))


def dot(a, b, dims=NN):
    return lax.dot_general(a, b, dims, preferred_element_type=F32)


def params(limit_mib):
    return pltpu.CompilerParams(vmem_limit_bytes=limit_mib * 2**20)


VMEM_MIB = 56
LIGHT = pl.CostEstimate(flops=1, bytes_accessed=1, transcendentals=0)


def pair_list(layers):
    return [(s, t) for s in range(layers) for t in range(s, layers)]


def gather_table(chips):
    table = np.full((2 * chips, 2 * chips - 1, 2), -1, np.int32)
    for me in range(2 * chips):
        chip, core = divmod(me, 2)
        way = 1 - 2 * core
        places = [(chip, core)]
        places += [(chip - way * j, core) for j in range(1, chips)]
        places += [(chip + way * j, 1 - core) for j in range(1, chips)]
        for piece, (place, order) in enumerate(places):
            if 0 <= place < chips:
                for half in range(2):
                    table[me, piece, half] = 2 * place + (order ^ half)
    return table.reshape(2 * chips, -1)


def scatter_table(chips):
    table = np.zeros((2 * chips, 3, 2 * chips), np.int32)
    counts = np.zeros((2 * chips, 1), np.int32)
    last = 2 * (chips - 1)
    for me in range(2 * chips):
        chip, core = divmod(me, 2)
        way = 1 - 2 * core
        gives, keeps = [], []
        for dist in range(chips - 1, 0, -1):
            slot = 2 * (chips - 1 - dist)
            for half in range(2):
                if 0 <= chip - way * dist < chips:
                    gives.append((2 * (chip - way * dist) + ((1 - core) ^ half), slot + half))
                if 0 <= chip + way * dist < chips:
                    keeps.append((2 * (chip + way * dist) + (core ^ half), slot + half))
        gives.append((2 * chip + 1 - core, last))
        keeps.append((2 * chip + core, last))
        for step, (tile, slot) in enumerate(gives):
            table[me, :, step] = (tile, slot, keeps[0][1])
        for step, (tile, slot) in enumerate(keeps):
            table[me, :, len(gives) + step] = (tile, gives[-1][1], slot)
        counts[me] = len(gives)
    return np.concatenate([table.reshape(2 * chips, -1), counts], 1)


def encode_kernel(res_ref, weight_ref, bias_ref, active_ref, out_ref):
    pre = dot(res_ref[0], weight_ref[0]) + bias_ref[pl.ds(pl.program_id(0), 1)]
    out_ref[0] = (pre * active_ref[0].astype(F32)).astype(BF16)


def encode(residual, enc_weight, bias, active, start, rows):
    layers, _, width = residual.shape
    own = enc_weight.shape[2]
    block = math.gcd(start, rows)
    at = start // block
    return pl.pallas_call(
        encode_kernel,
        grid=(layers, rows // block),
        in_specs=[
            pl.BlockSpec((1, block, width), lambda s, r: (s, at + r, 0)),
            pl.BlockSpec((1, width, own), lambda s, r: (s, 0, 0)),
            pl.BlockSpec((layers, own), lambda s, r: (0, 0)),
            pl.BlockSpec((1, block, own), lambda s, r: (s, at + r, 0)),
        ],
        out_specs=pl.BlockSpec((1, block, own), lambda s, r: (s, r, 0)),
        out_shape=jax.ShapeDtypeStruct((layers, rows, own), BF16),
        compiler_params=params(VMEM_MIB),
        cost_estimate=LIGHT,
        name="encode",
    )(residual, enc_weight, bias, active)


def recon_sum(pairs, weights, lat_tile, total):
    for t in range(total.shape[0]):
        term = total[t]
        for p, (source, target) in enumerate(pairs):
            if target == t:
                term = term + dot(weights[p][0], lat_tile(source), NT)
        total[t] = term


def recon_ends(low_ref, high_ref, total):
    @pl.when(pl.program_id(0) == pl.num_programs(0) - 1)
    def _():
        half = low_ref.shape[0]
        low_ref[...] = total[:half].astype(BF16)
        high_ref[...] = total[half:].astype(BF16)


def recon_whole_kernel(pairs, meta, *refs):
    weights = refs[: len(pairs)]
    lat_ref, low_ref, high_ref, total = refs[len(pairs) :]

    @pl.when(pl.program_id(0) == 0)
    def _():
        total[...] = jnp.zeros_like(total)

    recon_sum(pairs, weights, lambda source: lat_ref[0, source], total)
    recon_ends(low_ref, high_ref, total)


def recon_pieces_kernel(pairs, pieces, meta, *refs):
    npairs = len(pairs)
    weights = refs[:npairs]
    piece_refs = refs[npairs : npairs + pieces]
    low_ref, high_ref, lat_out, lat, total, in_sem, out_sem = refs[npairs + pieces :]
    step = pl.program_id(0)

    def fetch(piece, half):
        slot = meta[npairs + 2 * piece + half]
        return slot, pltpu.make_async_copy(
            piece_refs[piece].at[half], lat.at[jnp.maximum(slot, 0)], in_sem.at[2 * piece + half]
        )

    def keep():
        return pltpu.make_async_copy(lat, lat_out, out_sem)

    @pl.when(step == 0)
    def _():
        for piece in range(pieces):
            for half in range(2):
                slot, copy = fetch(piece, half)
                pl.when(slot >= 0)(copy.start)
        total[...] = jnp.zeros_like(total)
        for piece in range(pieces):
            for half in range(2):
                slot, copy = fetch(piece, half)
                pl.when(slot >= 0)(copy.wait)
        keep().start()

    recon_sum(pairs, weights, lambda source: lat[step, source], total)
    recon_ends(low_ref, high_ref, total)

    @pl.when(step == pl.num_programs(0) - 1)
    def _():
        keep().wait()


def weight_specs(npairs, feat, own, column):
    return [
        pl.BlockSpec((1, feat, own), functools.partial(lambda p, i, meta: (meta[p], 0, column(i, meta)), p))
        for p in range(npairs)
    ]


def recon(meta, dec_weight, lat):
    npairs, feat, cols = dec_weight.shape
    gathered = not isinstance(lat, list)
    *_, layers, rows, own = lat.shape if gathered else lat[0].shape
    tiles = cols // own
    pairs = pair_list(layers)
    half = layers // 2
    any_spec = pl.BlockSpec(memory_space=pl.ANY)
    outs = [
        jax.ShapeDtypeStruct((half, feat, rows), BF16),
        jax.ShapeDtypeStruct((layers - half, feat, rows), BF16),
    ]
    out_specs = [pl.BlockSpec(o.shape, lambda i, meta: (0, 0, 0)) for o in outs]
    scratch = [pltpu.VMEM((layers, feat, rows), F32)]
    if gathered:
        body = functools.partial(recon_whole_kernel, pairs)
        lat_specs = [pl.BlockSpec((1, layers, rows, own), lambda i, meta: (i, 0, 0, 0))]
    else:
        body = functools.partial(recon_pieces_kernel, pairs, len(lat))
        lat_specs = [any_spec] * len(lat)
        outs.append(jax.ShapeDtypeStruct((tiles, layers, rows, own), BF16))
        out_specs.append(any_spec)
        scratch = (
            [pltpu.VMEM((tiles, layers, rows, own), BF16)]
            + scratch
            + [pltpu.SemaphoreType.DMA((2 * len(lat),)), pltpu.SemaphoreType.DMA]
        )
    return pl.pallas_call(
        body,
        grid_spec=pltpu.PrefetchScalarGridSpec(
            num_scalar_prefetch=1,
            grid=(tiles,),
            in_specs=weight_specs(npairs, feat, own, lambda i, meta: i) + lat_specs,
            out_specs=out_specs,
            scratch_shapes=scratch,
        ),
        out_shape=outs,
        compiler_params=params(VMEM_MIB),
        cost_estimate=LIGHT,
        name="recon",
    )(meta, *([dec_weight] * npairs), *([lat] if gathered else lat))


def grad_kernel(pairs, layers, split, meta, *refs):
    npairs = len(pairs)
    weights = refs[:npairs]
    low_ref, high_ref, bias_ref, target_ref = refs[npairs : npairs + 4]
    outs = refs[npairs + 4 : -3]
    error_out, error_t, error_rest = refs[-3:]
    step = pl.program_id(0)
    feat, rows = target_ref.shape[1:]
    main = feat // 256 * 256
    rest = feat - main

    @pl.when(step == 0)
    def _():
        half = low_ref.shape[0]
        for t in range(layers):
            whole = low_ref[t] if t < half else high_ref[t - half]
            error = (whole.astype(F32) + bias_ref[t] - target_ref[t].astype(F32)).astype(BF16)
            error_out[t] = error
            turned = error.astype(F32).T.astype(BF16)
            if main:
                error_t[t] = turned[:, :main]
            if rest:
                for s in range(layers):
                    piece = turned[:, main:]
                    error_rest[s, :, t * rest : (t + 1) * rest] = piece if t >= s else jnp.zeros_like(piece)

    tiles = []
    for s in range(layers):
        total = None
        mine = [(p, t) for p, (source, t) in enumerate(pairs) if source == s]
        if main:
            for p, t in mine:
                term = dot(error_t[t], weights[p][0, :main])
                total = term if total is None else total + term
        if rest:
            stack = [weights[p][0, main:] for p, _ in mine]
            term = dot(error_rest[s][:, s * rest :], jnp.concatenate(stack, 0))
            total = term if total is None else total + term
        tiles.append(total.astype(BF16))

    def write(out_ref):
        for s in range(layers):
            out_ref[0, s] = tiles[s]

    if split:
        gives = meta[npairs + 3 * pl.num_programs(0)]
        early = meta[npairs + pl.num_programs(0) + step] < 2
        pl.when((step < gives) & early)(functools.partial(write, outs[0]))
        pl.when((step < gives) & ~early)(functools.partial(write, outs[1]))
        pl.when(step >= gives)(functools.partial(write, outs[2]))
    else:
        write(outs[0])


def grad(meta, dec_weight, low, high, bias, targets, own, split):
    npairs, feat, cols = dec_weight.shape
    layers, _, rows = targets.shape
    tiles = cols // own
    pairs = pair_list(layers)
    main = feat // 256 * 256
    rest = feat - main
    block = (1, layers, rows, own)
    if split:
        outs = [jax.ShapeDtypeStruct((count, layers, rows, own), BF16) for count in (2, tiles - 3, tiles - 1)]
        out_specs = [
            pl.BlockSpec(block, lambda i, meta: (jnp.minimum(meta[npairs + tiles + i], 1), 0, 0, 0)),
            pl.BlockSpec(block, lambda i, meta: (jnp.maximum(meta[npairs + tiles + i] - 2, 0), 0, 0, 0)),
            pl.BlockSpec(block, lambda i, meta: (meta[npairs + 2 * tiles + i], 0, 0, 0)),
        ]
        column = lambda i, meta: meta[npairs + i]
    else:
        outs = [jax.ShapeDtypeStruct((tiles, layers, rows, own), BF16)]
        out_specs = [pl.BlockSpec(block, lambda i, meta: (i, 0, 0, 0))]
        column = lambda i, meta: i
    whole = lambda shape: pl.BlockSpec(shape, lambda i, meta: (0,) * len(shape))
    return pl.pallas_call(
        functools.partial(grad_kernel, pairs, layers, split),
        grid_spec=pltpu.PrefetchScalarGridSpec(
            num_scalar_prefetch=1,
            grid=(tiles,),
            in_specs=weight_specs(npairs, feat, own, column)
            + [
                whole(low.shape),
                whole(high.shape),
                whole(bias.shape),
                whole(targets.shape),
            ],
            out_specs=out_specs + [whole((layers, feat, rows))],
            scratch_shapes=[
                pltpu.VMEM((layers, rows, max(main, 128)), BF16),
                pltpu.VMEM((layers, rows, max(layers * rest, 128)), BF16),
            ],
        ),
        out_shape=outs + [jax.ShapeDtypeStruct((layers, feat, rows), BF16)],
        compiler_params=params(VMEM_MIB),
        cost_estimate=LIGHT,
        name="latent_grad",
    )(meta, *([dec_weight] * npairs), low, high, bias, targets)


def dec_grad_kernel(pairs, parts, perm, *refs):
    errors, lats, out_ref = refs[:parts], refs[parts : 2 * parts], refs[-1]
    for p, (source, target) in enumerate(pairs):
        total = None
        for error, lat in zip(errors, lats):
            term = dot(error[target], lat[0, source])
            total = term if total is None else total + term
        out_ref[perm[p]] = total.astype(BF16)


def decoder_grad(perm, errors, lats):
    layers, feat, _ = errors[0].shape
    tiles, _, _, own = lats[0].shape
    pairs = pair_list(layers)
    npairs = len(pairs)
    return pl.pallas_call(
        functools.partial(dec_grad_kernel, pairs, len(errors)),
        grid_spec=pltpu.PrefetchScalarGridSpec(
            num_scalar_prefetch=1,
            grid=(tiles,),
            in_specs=[pl.BlockSpec(e.shape, lambda i, m: (0, 0, 0)) for e in errors]
            + [pl.BlockSpec((1,) + lat.shape[1:], lambda i, m: (i, 0, 0, 0)) for lat in lats],
            out_specs=pl.BlockSpec((npairs, feat, own), lambda i, m: (0, 0, i)),
        ),
        out_shape=jax.ShapeDtypeStruct((npairs, feat, tiles * own), BF16),
        compiler_params=params(VMEM_MIB),
        cost_estimate=LIGHT,
        name="dec_grad",
    )(perm, *errors, *lats)


def enc_grad_kernel(parts, res_ref, *refs):
    last_ref, active_ref, out_ref, bias_ref, whole = refs[parts:]

    @pl.when(pl.program_id(1) == 0)
    def _():
        last = (last_ref[0].astype(F32) * active_ref[...].astype(F32)).astype(BF16)
        value = jnp.concatenate([part[0] for part in refs[:parts]] + [last], 0)
        whole[...] = value
        bias_ref[pl.ds(pl.program_id(0), 1)] = jnp.sum(value.astype(F32), axis=0, keepdims=True)

    out_ref[0] = dot(res_ref[0], whole[...]).astype(BF16)


def encoder_grad(residual_t, grads, last, active, start):
    layers, width, tok = residual_t.shape
    _, rows, own = last.shape
    part = lambda value: pl.BlockSpec((1,) + value.shape[1:], lambda s, w: (s, 0, 0))
    return pl.pallas_call(
        functools.partial(enc_grad_kernel, len(grads)),
        grid=(layers, 1),
        in_specs=[pl.BlockSpec((1, width, tok), lambda s, w: (s, w, 0))]
        + [part(g) for g in grads]
        + [part(last), pl.BlockSpec((pl.Squeezed(), rows, own), lambda s, w: (s, 0, 0))],
        out_specs=[
            pl.BlockSpec((1, width, own), lambda s, w: (s, w, 0)),
            pl.BlockSpec((layers, own), lambda s, w: (0, 0)),
        ],
        out_shape=(
            jax.ShapeDtypeStruct((layers, width, own), BF16),
            jax.ShapeDtypeStruct((layers, own), F32),
        ),
        scratch_shapes=[pltpu.VMEM((tok, own), BF16)],
        compiler_params=params(VMEM_MIB),
        cost_estimate=LIGHT,
        name="enc_grad",
    )(residual_t, *grads, last, active[:, start : start + rows])


def swap_cores(value, devices):
    return lax.ppermute(value, "tgt", [(i, i ^ 1) for i in range(devices)])


def hop(value, chips, first):
    perm = []
    for chip in first:
        if chip + 1 < chips:
            perm.append((2 * chip, 2 * chip + 2))
            other = chips - 1 - chip
            perm.append((2 * other + 1, 2 * other - 1))
    return lax.ppermute(value, "tgt", perm)


def after(value, *others):
    return lax.optimization_barrier((value,) + others)[0]


def add(*values):
    total = values[0].astype(F32)
    for value in values[1:]:
        total = total + value.astype(F32)
    return total.astype(BF16)


def sum_over_src(value, size, bits):
    if size & (size - 1):
        return lax.psum(value, "src")
    for bit in bits:
        value = add(value, lax.ppermute(value, "src", [(i, i ^ (1 << bit)) for i in range(size)]))
    return value


def token_chunks(tok):
    parts = [2, 3, 3]
    unit = tok // sum(parts)
    return [(unit * sum(parts[:i]), unit * part) for i, part in enumerate(parts)]


def shards(blocks, devices, residual, targets, enc_weight, enc_bias, active, dec_weight, dec_bias, tile_pairs):
    layers, tok, _ = residual.shape
    own = enc_weight.shape[2]
    chips = devices // 2
    chunks = token_chunks(tok)
    hopping = 1
    pairs = np.array(pair_list(layers), np.int32)
    me = lax.axis_index("tgt")

    same = jnp.all(tile_pairs[None, :, :] == pairs[:, None, :], axis=2)
    perm = jnp.sum(jnp.where(same, jnp.arange(len(pairs), dtype=jnp.int32)[None, :], 0), axis=1, dtype=jnp.int32)
    scatter_meta = jnp.concatenate([perm, jnp.asarray(scatter_table(chips))[me]])
    dec_bias3 = dec_bias[:, :, None]
    residual_t = jnp.swapaxes(residual, 1, 2)
    bits = [b for b in range(blocks.bit_length()) if (1 << b) < blocks]

    def scatter(slots):
        early, rest, keep = slots
        early, rest = swap_cores(early, devices), swap_cores(rest, devices)
        last = 2 * (chips - 1)
        sent, carry = [], None
        for j in range(1, chips):
            at = slice(2 * (j - 1), 2 * j)
            terms = [keep[at], early if j == 1 else rest[2 * j - 4 : 2 * j - 2]]
            sent.append(add(*terms, *([] if carry is None else [carry])))
            carry = hop(sent[-1], chips, range(0, j))
        return sent, add(keep[last], rest[last - 2], carry[0], swap_cores(carry[1], devices))

    order, lats, parts = [], [], []
    for start, rows in chunks:
        block = encode(after(residual, *order), enc_weight, enc_bias, active, start, rows)
        order = [block]
        lats.append(lax.all_gather(block, "tgt", axis=0))
        parts.append(targets[:, :, start : start + rows])
    order += [residual_t, scatter_meta, dec_bias3] + parts

    errors, chains, totals = [], [], []
    for c in range(len(chunks)):
        stage = lambda ahead: [sent[min(2 * (c - i) - ahead, len(sent)) - 1] for i, (sent, _) in enumerate(chains)]
        low, high = recon(perm, dec_weight, after(lats[c], *order, *stage(1)))
        order = [low, high] + stage(0)
        low = sum_over_src(low, blocks, bits)
        high = sum_over_src(high, blocks, bits[::-1])
        split = c < hopping
        *slots, error = grad(scatter_meta, dec_weight, after(low, *order), high, dec_bias3, parts[c], own, split)
        errors.append(error)
        order = [error]
        if split:
            chains.append(scatter(slots))
            totals.append(chains[-1][1])
        else:
            totals.append(lax.psum_scatter(slots[0], "tgt", scatter_dimension=0))
    dec_grad = decoder_grad(after(perm, *order), errors, lats)
    grads = []
    for total, (start, rows) in zip(totals[:-1], chunks):
        grads.append((total.astype(F32) * active[:, start : start + rows].astype(F32)).astype(BF16))
    last = after(totals[-1], dec_grad, *grads)
    enc_grad, bias_grad = encoder_grad(residual_t, grads, last, active, chunks[-1][0])
    return (dec_grad, enc_grad, bias_grad)


def solution(mesh):
    in_specs = (
        P(),
        P(None, "tgt", None),
        P(None, None, ("src", "tgt")),
        P(None, ("src", "tgt")),
        P(None, None, ("src", "tgt")),
        P("src", "tgt", None),
        P(None, "tgt"),
        P("src", None),
    )
    out_specs = (P("src", "tgt", None), P(None, None, ("src", "tgt")), P(None, ("src", "tgt")))
    body = functools.partial(shards, mesh.shape["src"], mesh.shape["tgt"])
    return jax.shard_map(body, mesh=mesh, in_specs=in_specs, out_specs=out_specs, check_vma=False)
```

```python
import functools
import math

import jax
import jax.numpy as jnp
import numpy as np
from jax import lax
from jax.experimental import pallas as pl
from jax.experimental.pallas import tpu as pltpu
from jax.sharding import PartitionSpec as P

F32 = jnp.float32
BF16 = jnp.bfloat16
NT = (((1,), (1,)), ((), ()))
NN = (((1,), (0,)), ((), ()))


def dot(a, b, dims=NN):
    return lax.dot_general(a, b, dims, preferred_element_type=F32)


def params(limit_mib):
    return pltpu.CompilerParams(vmem_limit_bytes=limit_mib * 2**20)


VMEM_MIB = 56
LIGHT = pl.CostEstimate(flops=1, bytes_accessed=1, transcendentals=0)


def pair_list(layers):
    return [(s, t) for s in range(layers) for t in range(s, layers)]


def gather_table(chips):
    table = np.full((2 * chips, 2 * chips - 1, 2), -1, np.int32)
    for me in range(2 * chips):
        chip, core = divmod(me, 2)
        way = 1 - 2 * core
        places = [(chip, core)]
        places += [(chip - way * j, core) for j in range(1, chips)]
        places += [(chip + way * j, 1 - core) for j in range(1, chips)]
        for piece, (place, order) in enumerate(places):
            if 0 <= place < chips:
                for half in range(2):
                    table[me, piece, half] = 2 * place + (order ^ half)
    return table.reshape(2 * chips, -1)


def scatter_table(chips):
    table = np.zeros((2 * chips, 3, 2 * chips), np.int32)
    counts = np.zeros((2 * chips, 1), np.int32)
    last = 2 * (chips - 1)
    for me in range(2 * chips):
        chip, core = divmod(me, 2)
        way = 1 - 2 * core
        gives, keeps = [], []
        for dist in range(chips - 1, 0, -1):
            slot = 2 * (chips - 1 - dist)
            for half in range(2):
                if 0 <= chip - way * dist < chips:
                    gives.append((2 * (chip - way * dist) + ((1 - core) ^ half), slot + half))
                if 0 <= chip + way * dist < chips:
                    keeps.append((2 * (chip + way * dist) + (core ^ half), slot + half))
        gives.append((2 * chip + 1 - core, last))
        keeps.append((2 * chip + core, last))
        for step, (tile, slot) in enumerate(gives):
            table[me, :, step] = (tile, slot, keeps[0][1])
        for step, (tile, slot) in enumerate(keeps):
            table[me, :, len(gives) + step] = (tile, gives[-1][1], slot)
        counts[me] = len(gives)
    return np.concatenate([table.reshape(2 * chips, -1), counts], 1)


def encode_kernel(res_ref, weight_ref, bias_ref, active_ref, out_ref):
    pre = dot(res_ref[0], weight_ref[0]) + bias_ref[pl.ds(pl.program_id(0), 1)]
    out_ref[0] = (pre * active_ref[0].astype(F32)).astype(BF16)


def encode(residual, enc_weight, bias, active, start, rows):
    layers, _, width = residual.shape
    own = enc_weight.shape[2]
    block = math.gcd(start, rows)
    at = start // block
    return pl.pallas_call(
        encode_kernel,
        grid=(layers, rows // block),
        in_specs=[
            pl.BlockSpec((1, block, width), lambda s, r: (s, at + r, 0)),
            pl.BlockSpec((1, width, own), lambda s, r: (s, 0, 0)),
            pl.BlockSpec((layers, own), lambda s, r: (0, 0)),
            pl.BlockSpec((1, block, own), lambda s, r: (s, at + r, 0)),
        ],
        out_specs=pl.BlockSpec((1, block, own), lambda s, r: (s, r, 0)),
        out_shape=jax.ShapeDtypeStruct((layers, rows, own), BF16),
        compiler_params=params(VMEM_MIB),
        cost_estimate=LIGHT,
        name="encode",
    )(residual, enc_weight, bias, active)


def recon_sum(pairs, weights, lat_tile, total):
    for t in range(total.shape[0]):
        term = total[t]
        for p, (source, target) in enumerate(pairs):
            if target == t:
                term = term + dot(weights[p][0], lat_tile(source), NT)
        total[t] = term


def recon_ends(low_ref, high_ref, total):
    @pl.when(pl.program_id(0) == pl.num_programs(0) - 1)
    def _():
        half = low_ref.shape[0]
        low_ref[...] = total[:half].astype(BF16)
        high_ref[...] = total[half:].astype(BF16)


def recon_whole_kernel(pairs, meta, *refs):
    weights = refs[: len(pairs)]
    lat_ref, low_ref, high_ref, total = refs[len(pairs) :]

    @pl.when(pl.program_id(0) == 0)
    def _():
        total[...] = jnp.zeros_like(total)

    recon_sum(pairs, weights, lambda source: lat_ref[0, source], total)
    recon_ends(low_ref, high_ref, total)


def recon_pieces_kernel(pairs, pieces, meta, *refs):
    npairs = len(pairs)
    weights = refs[:npairs]
    piece_refs = refs[npairs : npairs + pieces]
    low_ref, high_ref, lat_out, lat, total, in_sem, out_sem = refs[npairs + pieces :]
    step = pl.program_id(0)

    def fetch(piece, half):
        slot = meta[npairs + 2 * piece + half]
        return slot, pltpu.make_async_copy(
            piece_refs[piece].at[half], lat.at[jnp.maximum(slot, 0)], in_sem.at[2 * piece + half]
        )

    def keep():
        return pltpu.make_async_copy(lat, lat_out, out_sem)

    @pl.when(step == 0)
    def _():
        for piece in range(pieces):
            for half in range(2):
                slot, copy = fetch(piece, half)
                pl.when(slot >= 0)(copy.start)
        total[...] = jnp.zeros_like(total)
        for piece in range(pieces):
            for half in range(2):
                slot, copy = fetch(piece, half)
                pl.when(slot >= 0)(copy.wait)
        keep().start()

    recon_sum(pairs, weights, lambda source: lat[step, source], total)
    recon_ends(low_ref, high_ref, total)

    @pl.when(step == pl.num_programs(0) - 1)
    def _():
        keep().wait()


def weight_specs(npairs, feat, own, column):
    return [
        pl.BlockSpec((1, feat, own), functools.partial(lambda p, i, meta: (meta[p], 0, column(i, meta)), p))
        for p in range(npairs)
    ]


def recon(meta, dec_weight, lat):
    npairs, feat, cols = dec_weight.shape
    gathered = not isinstance(lat, list)
    *_, layers, rows, own = lat.shape if gathered else lat[0].shape
    tiles = cols // own
    pairs = pair_list(layers)
    half = layers // 2
    any_spec = pl.BlockSpec(memory_space=pl.ANY)
    outs = [
        jax.ShapeDtypeStruct((half, feat, rows), BF16),
        jax.ShapeDtypeStruct((layers - half, feat, rows), BF16),
    ]
    out_specs = [pl.BlockSpec(o.shape, lambda i, meta: (0, 0, 0)) for o in outs]
    scratch = [pltpu.VMEM((layers, feat, rows), F32)]
    if gathered:
        body = functools.partial(recon_whole_kernel, pairs)
        lat_specs = [pl.BlockSpec((1, layers, rows, own), lambda i, meta: (i, 0, 0, 0))]
    else:
        body = functools.partial(recon_pieces_kernel, pairs, len(lat))
        lat_specs = [any_spec] * len(lat)
        outs.append(jax.ShapeDtypeStruct((tiles, layers, rows, own), BF16))
        out_specs.append(any_spec)
        scratch = (
            [pltpu.VMEM((tiles, layers, rows, own), BF16)]
            + scratch
            + [pltpu.SemaphoreType.DMA((2 * len(lat),)), pltpu.SemaphoreType.DMA]
        )
    return pl.pallas_call(
        body,
        grid_spec=pltpu.PrefetchScalarGridSpec(
            num_scalar_prefetch=1,
            grid=(tiles,),
            in_specs=weight_specs(npairs, feat, own, lambda i, meta: i) + lat_specs,
            out_specs=out_specs,
            scratch_shapes=scratch,
        ),
        out_shape=outs,
        compiler_params=params(VMEM_MIB),
        cost_estimate=LIGHT,
        name="recon",
    )(meta, *([dec_weight] * npairs), *([lat] if gathered else lat))


def grad_kernel(pairs, layers, split, meta, *refs):
    npairs = len(pairs)
    weights = refs[:npairs]
    low_ref, high_ref, bias_ref, target_ref = refs[npairs : npairs + 4]
    outs = refs[npairs + 4 : -3]
    error_out, error_t, error_rest = refs[-3:]
    step = pl.program_id(0)
    feat, rows = target_ref.shape[1:]
    main = feat // 256 * 256
    rest = feat - main

    @pl.when(step == 0)
    def _():
        half = low_ref.shape[0]
        for t in range(layers):
            whole = low_ref[t] if t < half else high_ref[t - half]
            error = (whole.astype(F32) + bias_ref[t] - target_ref[t].astype(F32)).astype(BF16)
            error_out[t] = error
            turned = error.astype(F32).T.astype(BF16)
            if main:
                error_t[t] = turned[:, :main]
            if rest:
                for s in range(layers):
                    piece = turned[:, main:]
                    error_rest[s, :, t * rest : (t + 1) * rest] = piece if t >= s else jnp.zeros_like(piece)

    tiles = []
    for s in range(layers):
        total = None
        mine = [(p, t) for p, (source, t) in enumerate(pairs) if source == s]
        if main:
            for p, t in mine:
                term = dot(error_t[t], weights[p][0, :main])
                total = term if total is None else total + term
        if rest:
            stack = [weights[p][0, main:] for p, _ in mine]
            term = dot(error_rest[s][:, s * rest :], jnp.concatenate(stack, 0))
            total = term if total is None else total + term
        tiles.append(total.astype(BF16))

    def write(out_ref):
        for s in range(layers):
            out_ref[0, s] = tiles[s]

    if split:
        gives = meta[npairs + 3 * pl.num_programs(0)]
        early = meta[npairs + pl.num_programs(0) + step] < 2
        pl.when((step < gives) & early)(functools.partial(write, outs[0]))
        pl.when((step < gives) & ~early)(functools.partial(write, outs[1]))
        pl.when(step >= gives)(functools.partial(write, outs[2]))
    else:
        write(outs[0])


def grad(meta, dec_weight, low, high, bias, targets, own, split):
    npairs, feat, cols = dec_weight.shape
    layers, _, rows = targets.shape
    tiles = cols // own
    pairs = pair_list(layers)
    main = feat // 256 * 256
    rest = feat - main
    block = (1, layers, rows, own)
    if split:
        outs = [jax.ShapeDtypeStruct((count, layers, rows, own), BF16) for count in (2, tiles - 3, tiles - 1)]
        out_specs = [
            pl.BlockSpec(block, lambda i, meta: (jnp.minimum(meta[npairs + tiles + i], 1), 0, 0, 0)),
            pl.BlockSpec(block, lambda i, meta: (jnp.maximum(meta[npairs + tiles + i] - 2, 0), 0, 0, 0)),
            pl.BlockSpec(block, lambda i, meta: (meta[npairs + 2 * tiles + i], 0, 0, 0)),
        ]
        column = lambda i, meta: meta[npairs + i]
    else:
        outs = [jax.ShapeDtypeStruct((tiles, layers, rows, own), BF16)]
        out_specs = [pl.BlockSpec(block, lambda i, meta: (i, 0, 0, 0))]
        column = lambda i, meta: i
    whole = lambda shape: pl.BlockSpec(shape, lambda i, meta: (0,) * len(shape))
    return pl.pallas_call(
        functools.partial(grad_kernel, pairs, layers, split),
        grid_spec=pltpu.PrefetchScalarGridSpec(
            num_scalar_prefetch=1,
            grid=(tiles,),
            in_specs=weight_specs(npairs, feat, own, column)
            + [
                whole(low.shape),
                whole(high.shape),
                whole(bias.shape),
                whole(targets.shape),
            ],
            out_specs=out_specs + [whole((layers, feat, rows))],
            scratch_shapes=[
                pltpu.VMEM((layers, rows, max(main, 128)), BF16),
                pltpu.VMEM((layers, rows, max(layers * rest, 128)), BF16),
            ],
        ),
        out_shape=outs + [jax.ShapeDtypeStruct((layers, feat, rows), BF16)],
        compiler_params=params(VMEM_MIB),
        cost_estimate=LIGHT,
        name="latent_grad",
    )(meta, *([dec_weight] * npairs), low, high, bias, targets)


def dec_grad_kernel(pairs, parts, perm, *refs):
    errors, lats, out_ref = refs[:parts], refs[parts : 2 * parts], refs[-1]
    for p, (source, target) in enumerate(pairs):
        total = None
        for error, lat in zip(errors, lats):
            term = dot(error[target], lat[0, source])
            total = term if total is None else total + term
        out_ref[perm[p]] = total.astype(BF16)


def decoder_grad(perm, errors, lats):
    layers, feat, _ = errors[0].shape
    tiles, _, _, own = lats[0].shape
    pairs = pair_list(layers)
    npairs = len(pairs)
    return pl.pallas_call(
        functools.partial(dec_grad_kernel, pairs, len(errors)),
        grid_spec=pltpu.PrefetchScalarGridSpec(
            num_scalar_prefetch=1,
            grid=(tiles,),
            in_specs=[pl.BlockSpec(e.shape, lambda i, m: (0, 0, 0)) for e in errors]
            + [pl.BlockSpec((1,) + lat.shape[1:], lambda i, m: (i, 0, 0, 0)) for lat in lats],
            out_specs=pl.BlockSpec((npairs, feat, own), lambda i, m: (0, 0, i)),
        ),
        out_shape=jax.ShapeDtypeStruct((npairs, feat, tiles * own), BF16),
        compiler_params=params(VMEM_MIB),
        cost_estimate=LIGHT,
        name="dec_grad",
    )(perm, *errors, *lats)


def enc_grad_kernel(parts, res_ref, *refs):
    last_ref, active_ref, out_ref, bias_ref, whole = refs[parts:]

    @pl.when(pl.program_id(1) == 0)
    def _():
        last = (last_ref[0].astype(F32) * active_ref[...].astype(F32)).astype(BF16)
        value = jnp.concatenate([part[0] for part in refs[:parts]] + [last], 0)
        whole[...] = value
        bias_ref[pl.ds(pl.program_id(0), 1)] = jnp.sum(value.astype(F32), axis=0, keepdims=True)

    out_ref[0] = dot(res_ref[0], whole[...]).astype(BF16)


def encoder_grad(residual_t, grads, last, active, start):
    layers, width, tok = residual_t.shape
    _, rows, own = last.shape
    part = lambda value: pl.BlockSpec((1,) + value.shape[1:], lambda s, w: (s, 0, 0))
    return pl.pallas_call(
        functools.partial(enc_grad_kernel, len(grads)),
        grid=(layers, 1),
        in_specs=[pl.BlockSpec((1, width, tok), lambda s, w: (s, w, 0))]
        + [part(g) for g in grads]
        + [part(last), pl.BlockSpec((pl.Squeezed(), rows, own), lambda s, w: (s, 0, 0))],
        out_specs=[
            pl.BlockSpec((1, width, own), lambda s, w: (s, w, 0)),
            pl.BlockSpec((layers, own), lambda s, w: (0, 0)),
        ],
        out_shape=(
            jax.ShapeDtypeStruct((layers, width, own), BF16),
            jax.ShapeDtypeStruct((layers, own), F32),
        ),
        scratch_shapes=[pltpu.VMEM((tok, own), BF16)],
        compiler_params=params(VMEM_MIB),
        cost_estimate=LIGHT,
        name="enc_grad",
    )(residual_t, *grads, last, active[:, start : start + rows])


def swap_cores(value, devices):
    return lax.ppermute(value, "tgt", [(i, i ^ 1) for i in range(devices)])


def hop(value, chips, first):
    perm = []
    for chip in first:
        if chip + 1 < chips:
            perm.append((2 * chip, 2 * chip + 2))
            other = chips - 1 - chip
            perm.append((2 * other + 1, 2 * other - 1))
    return lax.ppermute(value, "tgt", perm)


def far(value, chips, distance):
    perm = [(2 * chip, 2 * (chip + distance)) for chip in range(chips - distance)]
    perm += [(2 * chip + 1, 2 * (chip - distance) + 1) for chip in range(distance, chips)]
    return lax.ppermute(value, "tgt", perm)


def after(value, *others):
    return lax.optimization_barrier((value,) + others)[0]


def add(*values):
    total = values[0].astype(F32)
    for value in values[1:]:
        total = total + value.astype(F32)
    return total.astype(BF16)


def sum_over_src(value, size, bits):
    if size & (size - 1):
        return lax.psum(value, "src")
    for bit in bits:
        value = add(value, lax.ppermute(value, "src", [(i, i ^ (1 << bit)) for i in range(size)]))
    return value


def token_chunks(tok):
    parts = [2, 3, 3]
    unit = tok // sum(parts)
    return [(unit * sum(parts[:i]), unit * part) for i, part in enumerate(parts)]


def shards(blocks, devices, residual, targets, enc_weight, enc_bias, active, dec_weight, dec_bias, tile_pairs):
    layers, tok, _ = residual.shape
    own = enc_weight.shape[2]
    chips = devices // 2
    chunks = token_chunks(tok)
    hopping = 1
    pairs = np.array(pair_list(layers), np.int32)
    me = lax.axis_index("tgt")

    same = jnp.all(tile_pairs[None, :, :] == pairs[:, None, :], axis=2)
    perm = jnp.sum(jnp.where(same, jnp.arange(len(pairs), dtype=jnp.int32)[None, :], 0), axis=1, dtype=jnp.int32)
    scatter_meta = jnp.concatenate([perm, jnp.asarray(scatter_table(chips))[me]])
    dec_bias3 = dec_bias[:, :, None]
    residual_t = jnp.swapaxes(residual, 1, 2)
    bits = [b for b in range(blocks.bit_length()) if (1 << b) < blocks]

    def scatter(slots):
        early, rest, keep = slots
        early, rest = swap_cores(early, devices), swap_cores(rest, devices)
        last = 2 * (chips - 1)
        sent, come = [], []
        for j in range(1, chips):
            at = slice(2 * (j - 1), 2 * j)
            sent.append(add(keep[at], early if j == 1 else rest[2 * j - 4 : 2 * j - 2]))
            come.append(far(sent[-1], chips, chips - j))
        others = swap_cores(add(*[value[1] for value in come]), devices)
        return sent, add(keep[last], rest[last - 2], others, *[value[0] for value in come])

    order, lats, parts = [], [], []
    for start, rows in chunks:
        block = encode(after(residual, *order), enc_weight, enc_bias, active, start, rows)
        order = [block]
        lats.append(lax.all_gather(block, "tgt", axis=0))
        parts.append(targets[:, :, start : start + rows])
    order += [residual_t, scatter_meta, dec_bias3] + parts

    errors, chains, totals = [], [], []
    for c in range(len(chunks)):
        low, high = recon(perm, dec_weight, after(lats[c], *order, *[sent[0] for sent, _ in chains]))
        order = [low, high] + [value for sent, _ in chains for value in sent]
        low = sum_over_src(low, blocks, bits)
        high = sum_over_src(high, blocks, bits[::-1])
        split = c < hopping
        *slots, error = grad(scatter_meta, dec_weight, after(low, *order), high, dec_bias3, parts[c], own, split)
        errors.append(error)
        order = [error]
        if split:
            chains.append(scatter(slots))
            totals.append(chains[-1][1])
        else:
            totals.append(lax.psum_scatter(slots[0], "tgt", scatter_dimension=0))
    dec_grad = decoder_grad(after(perm, *order), errors, lats)
    grads = []
    for total, (start, rows) in zip(totals[:-1], chunks):
        grads.append((total.astype(F32) * active[:, start : start + rows].astype(F32)).astype(BF16))
    last = after(totals[-1], dec_grad, *grads)
    enc_grad, bias_grad = encoder_grad(residual_t, grads, last, active, chunks[-1][0])
    return (dec_grad, enc_grad, bias_grad)


def solution(mesh):
    in_specs = (
        P(),
        P(None, "tgt", None),
        P(None, None, ("src", "tgt")),
        P(None, ("src", "tgt")),
        P(None, None, ("src", "tgt")),
        P("src", "tgt", None),
        P(None, "tgt"),
        P("src", None),
    )
    out_specs = (P("src", "tgt", None), P(None, None, ("src", "tgt")), P(None, ("src", "tgt")))
    body = functools.partial(shards, mesh.shape["src"], mesh.shape["tgt"])
    return jax.shard_map(body, mesh=mesh, in_specs=in_specs, out_specs=out_specs, check_vma=False)
```
